1024 devices in a mesh: ab: 128 (over y, z), cd: 8 (over x, core).
Axes of the slice: x: 4, y: 8, z: 16, core: 2. Of those that a mesh axis runs over, the one named last changes fastest.
Arguments:
- amplitudes: bfloat16 [2, 1024, 14336], P(None, 'ab', 'cd'), may hold values from -6 to 6
- integrals: bfloat16 [8, 14336, 14336], P(None, 'ab', 'cd'), may hold values from -0.046875 to 0.046875
- batch_irrep: int32 [2], replicated, may hold values from 0 to 7
- pair_fill: int32 [8], replicated, may hold values from 7168 to 14336
Outputs:
- residual: float32 [2, 1024, 14336], P(None, 'cd', 'ab')
The draws below stay inside these ranges and needn't reach their ends.
All inputs are finite; a program needn't handle non-finite values.
Results may differ from the reference program's by a relative error of at most 0.00035.
Values may be sent and summed in bfloat16 or wider, within the bound.
No kernel may reach another device: no remote copies, remote signals or barrier semaphores. Data moves between devices by JAX's collectives and lax.ppermute only.
A program may use at most 32 MiB of HBM per device.

```python
import jax
import jax.numpy as jnp
from jax import lax

IRREPS = 8
BATCHES = 2
PB = 1024
VP = 14336
N_AB = 128


def touch_ends(array, rng, smallest, top_value):
    longest = array.shape.index(max(array.shape))
    spots = []
    for shift in (0, 1):
        where = [jax.random.randint(jax.random.fold_in(rng, axis), (), 0, length) for axis, length in enumerate(array.shape)]
        where[longest] = (where[longest] + shift) % array.shape[longest]
        spots.append(tuple(where))
    return array.at[spots[0]].set(smallest).at[spots[1]].set(top_value)


def block_scale(rng, dims, pieces, least, top_value):
    def one(axis_at, blocks):
        steps = jax.random.uniform(jax.random.fold_in(jax.random.fold_in(rng, 6), axis_at), (blocks,), jnp.float32, least / len(pieces), top_value / len(pieces))
        return jnp.repeat(jnp.exp(steps), dims[axis_at] // blocks).reshape((-1,) + (1,) * (len(dims) - axis_at - 1))

    gain = one(*pieces[0])
    for cut in pieces[1:]:
        gain = gain * one(*cut)
    return gain


def centred(own_key, dims, deviation, most, shards=(), kind=jnp.bfloat16):
    drawn = jax.random.normal(own_key, dims, jnp.float32) * deviation
    if len(shards) > 0:
        drawn = block_scale(own_key, dims, shards, -0.22, 0.18) * drawn
    return jnp.clip(drawn, min=-most, max=most).astype(kind)


def setup_inputs(seed: int = 0) -> dict:
    streams_of = jax.random.split(jax.random.key(seed), 5)
    return {
        "amplitudes": centred(streams_of[0], (BATCHES, PB, VP), 1.0, 6.0, ((1, 128), (2, 8))),
        "integrals": centred(streams_of[1], (IRREPS, VP, VP), VP ** -0.5, 0.046875, ((1, 128), (2, 8))),
        "batch_irrep": jax.random.randint(streams_of[2], (BATCHES,), 0, IRREPS).astype(jnp.int32),
        "pair_fill": touch_ends(jax.random.randint(streams_of[3], (IRREPS,), VP // 2, VP + 1), jax.random.fold_in(streams_of[3], 1), VP // 2, VP).astype(jnp.int32),
    }


def reference(amplitudes, integrals, batch_irrep, pair_fill):
    batches, pairs, columns = amplitudes.shape
    rows_all = integrals.shape[1]
    block_rows = rows_all // N_AB
    col_pos = jnp.arange(columns, dtype=jnp.int32)
    row_pos = jnp.arange(rows_all, dtype=jnp.int32)
    starts = jnp.arange(N_AB, dtype=jnp.int32) * block_rows
    results = []
    for batch in range(batches):
        irrep = batch_irrep[batch]
        limit = pair_fill[irrep]
        col_used = col_pos < limit
        row_used = row_pos < limit
        masked = jnp.where(col_used[None, :], amplitudes[batch], jnp.zeros((), amplitudes.dtype))

        def one_block(start):
            block = lax.dynamic_slice(integrals, (irrep.astype(jnp.int32), start.astype(jnp.int32), jnp.zeros((), jnp.int32)), (1, block_rows, columns))[0]
            return jnp.dot(masked, block.T, preferred_element_type=jnp.float32)

        parts = lax.map(one_block, starts)
        ladder = jnp.transpose(parts, (1, 0, 2)).reshape(pairs, rows_all)
        results.append(jnp.where(row_used[None, :], ladder, jnp.zeros((), ladder.dtype)))
    return jnp.stack(results)
```

```python
import jax
import jax.numpy as jnp
from jax import lax
from jax.experimental import pallas as pl
from jax.experimental.pallas import tpu as pltpu
from jax.sharding import Mesh, PartitionSpec as P

Y, ZA, ZB, X, C = 8, 4, 4, 4, 2
Z = ZA * ZB
ZAX = ("za", "zb")
LANES = 128
OFFSETS = (0, -1, 1, -2, 2, -3, 3, 4)


def shift(values, axis, size, step):
    return lax.ppermute(values, axis, [(i, (i + step) % size) for i in range(size)])


def swap_cores(values):
    return lax.ppermute(values, "c", [(0, 1), (1, 0)])


def pick_kernel(irrep_ref, integrals_ref, mine_ref, other_ref, sems):
    core = lax.axis_index("c")
    mine = pltpu.make_async_copy(integrals_ref.at[irrep_ref[core]], mine_ref, sems.at[0])
    other = pltpu.make_async_copy(integrals_ref.at[irrep_ref[1 - core]], other_ref, sems.at[1])
    mine.start()
    other.start()
    mine.wait()
    other.wait()


def pick(batch_irrep, integrals):
    block = jax.ShapeDtypeStruct(integrals.shape[1:], integrals.dtype)
    return pl.pallas_call(
        pick_kernel,
        out_shape=(block, block),
        in_specs=[pl.BlockSpec(memory_space=pltpu.SMEM), pl.BlockSpec(memory_space=pl.ANY)],
        out_specs=[pl.BlockSpec(memory_space=pltpu.VMEM)] * 2,
        scratch_shapes=[pltpu.SemaphoreType.DMA((2,))],
        cost_estimate=pl.CostEstimate(flops=0, bytes_accessed=2**21, transcendentals=0),
        name="pick_blocks",
    )(batch_irrep, integrals)


def ladder_kernel(irrep_ref, fill_ref, *refs):
    pairs, blocks = refs[: len(OFFSETS)], refs[len(OFFSETS) : len(OFFSETS) + 4]
    out_ref, left, right, left_sems, right_sems = refs[len(OFFSETS) + 4 :]
    halves, rows, cols = pairs[0].shape
    ab_rows = blocks[0].shape[1]
    y, x, core = lax.axis_index("y"), lax.axis_index("x"), lax.axis_index("c")

    left_loads = [
        pltpu.make_async_copy(
            pair.at[half], left.at[at, :, pl.ds(half * cols, cols)], left_sems.at[at, half]
        )
        for at, pair in enumerate(pairs)
        for half in range(halves)
    ]
    places = [pl.multiple_of(lax.rem(core + half, halves) * cols, LANES) for half in range(halves)]
    right_loads = [
        [
            pltpu.make_async_copy(
                block.at[half], right.at[at, pl.ds(0, ab_rows), pl.ds(places[half], cols)], right_sems.at[at, half]
            )
            for half in range(halves)
        ]
        for at, block in enumerate(blocks)
    ]
    for load in left_loads + right_loads[0] + right_loads[1] + right_loads[2] + right_loads[3]:
        load.start()
    for load in left_loads:
        load.wait()
    limit = fill_ref[irrep_ref[core]]
    place = x * halves * cols + lax.broadcasted_iota(jnp.int32, (1, halves * cols), 1)
    every = left[...].reshape(len(pairs) * rows, halves * cols)
    every = jnp.where(place < limit, every, jnp.zeros((), every.dtype))
    for pair in range(2):
        for load in right_loads[2 * pair] + right_loads[2 * pair + 1]:
            load.wait()
        weight = right[pl.ds(2 * pair, 2)].reshape(2 * LANES, halves * cols)
        product = lax.dot_general(
            every, weight, (((1,), (1,)), ((), ())), preferred_element_type=jnp.float32
        )
        for at, offset in enumerate(OFFSETS):
            owner = lax.rem(y + offset + Y, Y)
            for part in range(2):
                out_ref[owner, 2 * pair + part] = product[
                    at * rows : (at + 1) * rows, part * LANES : part * LANES + ab_rows
                ]


def partial_ladder(batch_irrep, pair_fill, pairs, blocks):
    halves, rows, cols = pairs[0].shape
    owners, ab_rows = len(pairs), blocks[0].shape[1]
    flops = 2 * owners * rows * 4 * ab_rows * halves * cols
    return pl.pallas_call(
        ladder_kernel,
        out_shape=jax.ShapeDtypeStruct((owners, 4, rows, ab_rows), jnp.float32),
        in_specs=[pl.BlockSpec(memory_space=pltpu.SMEM)] * 2
        + [pl.BlockSpec(memory_space=pl.ANY)] * (owners + 4),
        out_specs=pl.BlockSpec(memory_space=pltpu.VMEM),
        scratch_shapes=[
            pltpu.VMEM((owners, rows, halves * cols), jnp.bfloat16),
            pltpu.VMEM((4, LANES, halves * cols), jnp.bfloat16),
            pltpu.SemaphoreType.DMA((owners, halves)),
            pltpu.SemaphoreType.DMA((4, halves)),
        ],
        compiler_params=pltpu.CompilerParams(vmem_limit_bytes=56 * 2**20),
        cost_estimate=pl.CostEstimate(flops=flops, bytes_accessed=6 * 2**20, transcendentals=0),
        name="partial_ladder",
    )(batch_irrep, pair_fill, *pairs, *blocks)


def on_device(amplitudes, integrals, batch_irrep, pair_fill):
    batches, own_pairs, cd_cols = amplitudes.shape
    ab_rows = integrals.shape[1]
    y_place = lax.axis_index("y")
    z_place = lax.axis_index(ZAX)
    limits = pair_fill[batch_irrep]

    def of_batch(values, n):
        return lax.dynamic_index_in_dim(values, n, 0, keepdims=False)

    mine, other = pick(batch_irrep, integrals)
    other = swap_cores(other)
    spread = jnp.broadcast_to(amplitudes[None], (ZA, *amplitudes.shape)).reshape(ZA * C, own_pairs, cd_cols)
    own = lax.all_to_all(spread, ("za", "c"), 0, 0, tiled=True)
    own = own.reshape(ZA, C, own_pairs, cd_cols).transpose(1, 0, 2, 3).reshape(C, ZA * own_pairs, cd_cols)
    mid = jnp.stack([mine, other])
    own, mid = lax.optimization_barrier((own, mid))

    low1 = shift(mid, ZAX, Z, 1)
    right1, left1 = shift(own, "y", Y, 1), shift(own, "y", Y, -1)
    right2, left2 = shift(right1, "y", Y, 1), shift(left1, "y", Y, -1)
    mid, left2 = lax.optimization_barrier((mid, left2))
    high1 = shift(mid, ZAX, Z, -1)
    right3, left3 = shift(right2, "y", Y, 1), shift(left2, "y", Y, -1)
    low1, right3 = lax.optimization_barrier((low1, right3))
    low2 = shift(low1, ZAX, Z, 1)
    right4 = shift(right3, "y", Y, 1)
    pairs = [own, right1, left1, right2, left2, right3, left3, right4]

    partial = partial_ladder(batch_irrep, pair_fill, pairs, [low2, low1, mid, high1])
    parts = lax.all_to_all(partial, ("x", "c"), 0, 0, tiled=True)
    total = jnp.sum(parts.reshape(X, C, *parts.shape[1:]), axis=0)

    pieces = jnp.stack(
        [
            total[:, 2],
            shift(total[:, 1], ZAX, Z, -1),
            shift(total[:, 0], ZAX, Z, -2),
            shift(total[:, 3], ZAX, Z, 1),
        ]
    )
    z_class = lax.rem(z_place, ZB)
    classes = [of_batch(pieces, lax.rem(b - z_class + ZB, ZB)) for b in range(ZB)]
    ladder = jnp.stack([piece.reshape(batches, ZA, own_pairs, ab_rows) for piece in classes], axis=2)
    ladder = ladder.reshape(batches, ZA * ZB * own_pairs, ab_rows)
    row_used = (y_place * Z + z_place) * ab_rows + jnp.arange(ab_rows, dtype=jnp.int32) < limits[:, None]
    return jnp.where(row_used[:, None, :], ladder, jnp.zeros((), jnp.float32))


def solution(mesh):
    whole = Mesh(mesh.devices.reshape(Y, ZA, ZB, X, C), ("y", "za", "zb", "x", "c"))
    placed = (P(None, ("y", "za", "zb"), ("x", "c")),) * 2 + (P(), P())
    return jax.shard_map(
        on_device,
        mesh=whole,
        in_specs=placed,
        out_specs=P(None, ("x", "c"), ("y", "za", "zb")),
        check_vma=False,
    )
```

```python
import jax
import jax.numpy as jnp
from jax import lax
from jax.experimental import pallas as pl
from jax.experimental.pallas import tpu as pltpu
from jax.sharding import Mesh, PartitionSpec as P

Y, ZA, H, PAR, X, C = 8, 4, 2, 2, 4, 2
AXES = ("y", "za", "h", "par", "x", "c")
QUAD = H * PAR
LANES = 128
TOP = 14


def trade(values, first):
    pairs = []
    for even in range(0, Y, 2):
        other = (even + 1 - 2 * first) % Y
        pairs += [(even, other), (other, even)]
    return lax.ppermute(values, "y", pairs)


def owner_of(y, part, at):
    step = (0, 1, -1, -2, 2, 3, -3, -4)[at]
    side = 1 - 2 * lax.rem(y + part, 2)
    return lax.rem(y + side * step + Y, Y)


def pick_kernel(irrep_ref, integrals_ref, out_ref, sems):
    cols = out_ref.shape[-1]
    copies = [
        pltpu.make_async_copy(
            integrals_ref.at[irrep_ref[n], :, pl.ds(h * cols, cols)], out_ref.at[h, par, n], sems.at[h, par, n]
        )
        for h in range(H)
        for par in range(PAR)
        for n in range(C)
    ]
    for copy in copies:
        copy.start()
    for copy in copies:
        copy.wait()


def pick(batch_irrep, integrals):
    ab_rows, cols = integrals.shape[1:]
    return pl.pallas_call(
        pick_kernel,
        out_shape=jax.ShapeDtypeStruct((H, PAR, C, ab_rows, cols // H), integrals.dtype),
        in_specs=[pl.BlockSpec(memory_space=pltpu.SMEM), pl.BlockSpec(memory_space=pl.ANY)],
        out_specs=pl.BlockSpec(memory_space=pltpu.VMEM),
        scratch_shapes=[pltpu.SemaphoreType.DMA((H, PAR, C))],
        cost_estimate=pl.CostEstimate(flops=0, bytes_accessed=2**21, transcendentals=0),
        name="pick_blocks",
    )(batch_irrep, integrals)


def ladder_kernel(irrep_ref, fill_ref, *refs):
    pairs, blocks_ref = refs[: 4 * C], refs[4 * C]
    out_ref, left, right = refs[4 * C + 1 :]
    _, rows, cols = pairs[0].shape
    parts, ab_rows = blocks_ref.shape[1:3]
    y, x, h, core = (lax.axis_index(axis) for axis in ("y", "x", "h", "c"))

    limit = fill_ref[irrep_ref[core]]
    for part in range(parts):
        place = ((x * C + part) * H + h) * cols + lax.broadcasted_iota(jnp.int32, (1, cols), 1)
        used = place < limit
        for at in range(Y):
            values = pairs[part * 4 + at // 2][at % 2]
            left[part, owner_of(y, part, at)] = jnp.where(used, values, jnp.zeros((), values.dtype))
    for at in range(QUAD):
        for part in range(parts):
            right[part, at, pl.ds(0, ab_rows)] = blocks_ref[at, part]
    column = lax.broadcasted_iota(jnp.int32, (1, LANES), 1)
    for half in range(QUAD // 2):
        product = sum(
            lax.dot_general(
                left[part].reshape(Y * rows, cols),
                right[part, pl.ds(2 * half, 2)].reshape(2 * LANES, cols),
                (((1,), (1,)), ((), ())),
                preferred_element_type=jnp.float32,
            )
            for part in range(parts)
        )
        for side in range(2):
            tile = product[:, side * LANES : (side + 1) * LANES]
            tile = jnp.where(column < ab_rows, tile, jnp.zeros((), jnp.float32))
            peak = jnp.max(jnp.abs(tile), axis=1, keepdims=True)
            power = jnp.clip(jnp.ceil(jnp.log2(jnp.maximum(peak, 1e-37))), -112.0, 112.0)
            scaled = jnp.where(column == ab_rows, power, tile * jnp.exp2(TOP - power))
            whole = jnp.floor(scaled + 0.5).astype(jnp.int32).astype(jnp.int16)
            out_ref[2 * half + side] = whole.reshape(Y, rows, LANES)


def total_kernel(irrep_ref, fill_ref, parts_ref, out_ref):
    batches, ab_rows, _ = out_ref.shape
    rows = parts_ref.shape[1]
    place = lax.axis_index("y")
    for axis, size in (("za", ZA), ("h", H), ("par", PAR)):
        place = place * size + lax.axis_index(axis)
    ab = place * ab_rows + lax.broadcasted_iota(jnp.int32, (ab_rows, 1), 0)
    for n in range(batches):
        classes = []
        for par in range(PAR):
            total = jnp.zeros((rows, LANES), jnp.float32)
            for h in range(H):
                for x in range(X):
                    part = parts_ref[((h * PAR + par) * X + x) * C + n].astype(jnp.float32)
                    total += part * jnp.exp2(part[:, ab_rows : ab_rows + 1] - TOP)
            classes.append(total)
        eight = rows // (ZA * H)
        pieces = [
            classes[par][at * eight : (at + 1) * eight] for at in range(ZA * H) for par in range(PAR)
        ]
        turned = jnp.concatenate(pieces, axis=0).T[:ab_rows]
        out_ref[n] = jnp.where(ab < fill_ref[irrep_ref[n]], turned, jnp.zeros((), jnp.float32))


def total_ladder(batch_irrep, pair_fill, parts, batches, ab_rows):
    return pl.pallas_call(
        total_kernel,
        out_shape=jax.ShapeDtypeStruct((batches, ab_rows, PAR * parts.shape[1]), jnp.float32),
        in_specs=[pl.BlockSpec(memory_space=pltpu.SMEM)] * 2 + [pl.BlockSpec(memory_space=pltpu.VMEM)],
        out_specs=pl.BlockSpec(memory_space=pltpu.VMEM),
        cost_estimate=pl.CostEstimate(flops=2**20, bytes_accessed=2**20, transcendentals=0),
        name="total_ladder",
    )(batch_irrep, pair_fill, parts)


def partial_ladder(batch_irrep, pair_fill, pairs, blocks):
    _, rows, cols = pairs[0].shape
    parts, ab_rows = blocks.shape[1:3]
    owners = Y
    flops = 2 * owners * rows * QUAD * ab_rows * parts * cols
    return pl.pallas_call(
        ladder_kernel,
        out_shape=jax.ShapeDtypeStruct((QUAD, owners, rows, LANES), jnp.int16),
        in_specs=[pl.BlockSpec(memory_space=pltpu.SMEM)] * 2
        + [pl.BlockSpec(memory_space=pltpu.VMEM)] * (len(pairs) + 1),
        out_specs=pl.BlockSpec(memory_space=pltpu.VMEM),
        scratch_shapes=[
            pltpu.VMEM((parts, owners, rows, cols), jnp.bfloat16),
            pltpu.VMEM((parts, QUAD, LANES, cols), jnp.bfloat16),
        ],
        compiler_params=pltpu.CompilerParams(vmem_limit_bytes=24 * 2**20),
        cost_estimate=pl.CostEstimate(flops=flops, bytes_accessed=6 * 2**20, transcendentals=0),
        name="partial_ladder",
    )(batch_irrep, pair_fill, *pairs, blocks)


def on_device(amplitudes, integrals, batch_irrep, pair_fill):
    batches, own_pairs, cd_cols = amplitudes.shape
    ab_rows = integrals.shape[1]
    cols = cd_cols // H

    spread = amplitudes.reshape(batches, own_pairs, H, cols).transpose(2, 0, 1, 3)
    spread = jnp.broadcast_to(spread[None], (ZA, H, C, own_pairs, cols)).reshape(-1, own_pairs, cols)
    own = lax.all_to_all(spread, ("za", "h", "c"), 0, 0, tiled=True)
    own = own.reshape(ZA, H, C, own_pairs, cols).transpose(2, 0, 1, 3, 4).reshape(C, ZA * H * own_pairs, cols)

    picked = pick(batch_irrep, integrals).reshape(-1, ab_rows, cols)
    blocks = lax.all_to_all(picked, ("h", "par", "c"), 0, 0, tiled=True).reshape(QUAD, C, ab_rows, cols)

    pairs = [[], []]
    held = [own[0][None], own[1][None]]
    for step in range(4):
        for part in range(C):
            came = trade(held[part], (step + part) % 2)
            if step == 0:
                came = jnp.concatenate([held[part], came], axis=0)
            held[part] = came
            pairs[part].append(came)
    pairs = pairs[0] + pairs[1]

    partial = partial_ladder(batch_irrep, pair_fill, pairs, blocks)
    partial = partial.reshape(-1, *partial.shape[2:])
    parts = lax.all_to_all(partial, ("h", "par", "x", "c"), 0, 0, tiled=True)
    return total_ladder(batch_irrep, pair_fill, parts, batches, ab_rows).swapaxes(1, 2)


def solution(mesh):
    whole = Mesh(mesh.devices.reshape(Y, ZA, H, PAR, X, C), AXES)
    placed = (P(None, AXES[:4], AXES[4:]),) * 2 + (P(), P())
    return jax.shard_map(
        on_device, mesh=whole, in_specs=placed, out_specs=P(None, AXES[4:], AXES[:4]), check_vma=False
    )
```

```python
import jax
import jax.numpy as jnp
from jax import lax
from jax.experimental import pallas as pl
from jax.experimental.pallas import tpu as pltpu
from jax.sharding import Mesh, PartitionSpec as P

Y, ZA, H, PAR, X, C = 8, 4, 2, 2, 4, 2
AXES = ("y", "za", "h", "par", "x", "c")
QUAD = H * PAR
LANES = 128
TOP = 15


def trade(values, first):
    pairs = []
    for even in range(0, Y, 2):
        other = (even + 1 - 2 * first) % Y
        pairs += [(even, other), (other, even)]
    return lax.ppermute(values, "y", pairs)


def owner_of(y, part, at):
    step = (0, 1, -1, -2, 2, 3, -3, -4)[at]
    side = 1 - 2 * lax.rem(y + part, 2)
    return lax.rem(y + side * step + Y, Y)


def pick_kernel(irrep_ref, integrals_ref, out_ref, sems):
    cols = out_ref.shape[-1]
    copies = [
        pltpu.make_async_copy(
            integrals_ref.at[irrep_ref[n], :, pl.ds(h * cols, cols)], out_ref.at[h, par, n], sems.at[h, par, n]
        )
        for h in range(H)
        for par in range(PAR)
        for n in range(C)
    ]
    for copy in copies:
        copy.start()
    for copy in copies:
        copy.wait()


def pick(batch_irrep, integrals):
    ab_rows, cols = integrals.shape[1:]
    return pl.pallas_call(
        pick_kernel,
        out_shape=jax.ShapeDtypeStruct((H, PAR, C, ab_rows, cols // H), integrals.dtype),
        in_specs=[pl.BlockSpec(memory_space=pltpu.SMEM), pl.BlockSpec(memory_space=pl.ANY)],
        out_specs=pl.BlockSpec(memory_space=pltpu.VMEM),
        scratch_shapes=[pltpu.SemaphoreType.DMA((H, PAR, C))],
        cost_estimate=pl.CostEstimate(flops=0, bytes_accessed=2**21, transcendentals=0),
        name="pick_blocks",
    )(batch_irrep, integrals)


def ladder_kernel(irrep_ref, fill_ref, *refs):
    pairs, blocks_ref = refs[: 4 * C], refs[4 * C]
    out_ref, left, right = refs[4 * C + 1 :]
    _, rows, cols = pairs[0].shape
    parts, ab_rows = blocks_ref.shape[1:3]
    y, x, h, core = (lax.axis_index(axis) for axis in ("y", "x", "h", "c"))

    limit = fill_ref[irrep_ref[core]]
    for part in range(parts):
        place = ((x * C + part) * H + h) * cols + lax.broadcasted_iota(jnp.int32, (1, cols), 1)
        used = place < limit
        for at in range(Y):
            values = pairs[part * 4 + at // 2][at % 2]
            left[part, owner_of(y, part, at)] = jnp.where(used, values, jnp.zeros((), values.dtype))
    for at in range(QUAD):
        for part in range(parts):
            right[part, at, pl.ds(0, ab_rows)] = blocks_ref[at, part]
    column = lax.broadcasted_iota(jnp.int32, (1, LANES), 1)
    for half in range(QUAD // 2):
        product = sum(
            lax.dot_general(
                left[part].reshape(Y * rows, cols),
                right[part, pl.ds(2 * half, 2)].reshape(2 * LANES, cols),
                (((1,), (1,)), ((), ())),
                preferred_element_type=jnp.float32,
            )
            for part in range(parts)
        )
        for side in range(2):
            tile = product[:, side * LANES : (side + 1) * LANES]
            tile = jnp.where(column < ab_rows, tile, jnp.zeros((), jnp.float32))
            peak = jnp.max(jnp.abs(tile), axis=1, keepdims=True)
            power = jnp.clip(jnp.ceil(jnp.log2(jnp.maximum(peak * 1.0001, 1e-37))), -111.0, 111.0)
            scaled = jnp.where(column == ab_rows, power, tile * jnp.exp2(TOP - power))
            whole = jnp.floor(scaled + 0.5).astype(jnp.int32).astype(jnp.int16)
            out_ref[2 * half + side] = whole.reshape(Y, rows, LANES)


def total_kernel(irrep_ref, fill_ref, parts_ref, out_ref):
    batches, ab_rows, _ = out_ref.shape
    rows = parts_ref.shape[1]
    place = lax.axis_index("y")
    for axis, size in (("za", ZA), ("h", H), ("par", PAR)):
        place = place * size + lax.axis_index(axis)
    ab = place * ab_rows + lax.broadcasted_iota(jnp.int32, (ab_rows, 1), 0)
    for n in range(batches):
        classes = []
        for par in range(PAR):
            total = jnp.zeros((rows, LANES), jnp.float32)
            for h in range(H):
                for x in range(X):
                    part = parts_ref[((h * PAR + par) * X + x) * C + n].astype(jnp.float32)
                    total += part * jnp.exp2(part[:, ab_rows : ab_rows + 1] - TOP)
            classes.append(total)
        eight = rows // (ZA * H)
        pieces = [
            classes[par][at * eight : (at + 1) * eight] for at in range(ZA * H) for par in range(PAR)
        ]
        turned = jnp.concatenate(pieces, axis=0).T[:ab_rows]
        out_ref[n] = jnp.where(ab < fill_ref[irrep_ref[n]], turned, jnp.zeros((), jnp.float32))


def total_ladder(batch_irrep, pair_fill, parts, batches, ab_rows):
    return pl.pallas_call(
        total_kernel,
        out_shape=jax.ShapeDtypeStruct((batches, ab_rows, PAR * parts.shape[1]), jnp.float32),
        in_specs=[pl.BlockSpec(memory_space=pltpu.SMEM)] * 2 + [pl.BlockSpec(memory_space=pltpu.VMEM)],
        out_specs=pl.BlockSpec(memory_space=pltpu.VMEM),
        cost_estimate=pl.CostEstimate(flops=2**20, bytes_accessed=2**20, transcendentals=0),
        name="total_ladder",
    )(batch_irrep, pair_fill, parts)


def partial_ladder(batch_irrep, pair_fill, pairs, blocks):
    _, rows, cols = pairs[0].shape
    parts, ab_rows = blocks.shape[1:3]
    owners = Y
    flops = 2 * owners * rows * QUAD * ab_rows * parts * cols
    return pl.pallas_call(
        ladder_kernel,
        out_shape=jax.ShapeDtypeStruct((QUAD, owners, rows, LANES), jnp.int16),
        in_specs=[pl.BlockSpec(memory_space=pltpu.SMEM)] * 2
        + [pl.BlockSpec(memory_space=pltpu.VMEM)] * (len(pairs) + 1),
        out_specs=pl.BlockSpec(memory_space=pltpu.VMEM),
        scratch_shapes=[
            pltpu.VMEM((parts, owners, rows, cols), jnp.bfloat16),
            pltpu.VMEM((parts, QUAD, LANES, cols), jnp.bfloat16),
        ],
        compiler_params=pltpu.CompilerParams(vmem_limit_bytes=24 * 2**20),
        cost_estimate=pl.CostEstimate(flops=flops, bytes_accessed=6 * 2**20, transcendentals=0),
        name="partial_ladder",
    )(batch_irrep, pair_fill, *pairs, blocks)


def on_device(amplitudes, integrals, batch_irrep, pair_fill):
    batches, own_pairs, cd_cols = amplitudes.shape
    ab_rows = integrals.shape[1]
    cols = cd_cols // H

    spread = amplitudes.reshape(batches, own_pairs, H, cols).transpose(2, 0, 1, 3)
    spread = jnp.broadcast_to(spread[None], (ZA, H, C, own_pairs, cols)).reshape(-1, own_pairs, cols)
    own = lax.all_to_all(spread, ("za", "h", "c"), 0, 0, tiled=True)
    own = own.reshape(ZA, H, C, own_pairs, cols).transpose(2, 0, 1, 3, 4).reshape(C, ZA * H * own_pairs, cols)

    picked = pick(batch_irrep, integrals).reshape(-1, ab_rows, cols)
    blocks = lax.all_to_all(picked, ("h", "par", "c"), 0, 0, tiled=True).reshape(QUAD, C, ab_rows, cols)

    pairs = [[], []]
    held = [own[0][None], own[1][None]]
    for step in range(4):
        for part in range(C):
            came = trade(held[part], (step + part) % 2)
            if step == 0:
                came = jnp.concatenate([held[part], came], axis=0)
            held[part] = came
            pairs[part].append(came)
    pairs = pairs[0] + pairs[1]

    partial = partial_ladder(batch_irrep, pair_fill, pairs, blocks)
    partial = partial.reshape(-1, *partial.shape[2:])
    parts = lax.all_to_all(partial, ("h", "par", "x", "c"), 0, 0, tiled=True)
    return total_ladder(batch_irrep, pair_fill, parts, batches, ab_rows).swapaxes(1, 2)


def solution(mesh):
    whole = Mesh(mesh.devices.reshape(Y, ZA, H, PAR, X, C), AXES)
    placed = (P(None, AXES[:4], AXES[4:]),) * 2 + (P(), P())
    return jax.shard_map(
        on_device, mesh=whole, in_specs=placed, out_specs=P(None, AXES[4:], AXES[:4]), check_vma=False
    )
```

```python
import jax
import jax.numpy as jnp
from jax import lax
from jax.experimental import pallas as pl
from jax.experimental.pallas import tpu as pltpu
from jax.sharding import Mesh, PartitionSpec as P

Y, ZA, H, PAR, X, C = 8, 4, 2, 2, 4, 2
AXES = ("y", "za", "h", "par", "x", "c")
QUAD = H * PAR
LANES = 128
TOP = 15


def trade(values, first):
    pairs = []
    for even in range(0, Y, 2):
        other = (even + 1 - 2 * first) % Y
        pairs += [(even, other), (other, even)]
    return lax.ppermute(values, "y", pairs)


def owner_of(y, part, at):
    step = (0, 1, -1, -2, 2, 3, -3, -4)[at]
    side = 1 - 2 * lax.rem(y + part, 2)
    return lax.rem(y + side * step + Y, Y)


def pick_kernel(irrep_ref, integrals_ref, out_ref, sems):
    cols = out_ref.shape[-1]
    copies = [
        pltpu.make_async_copy(
            integrals_ref.at[irrep_ref[n], :, pl.ds(h * cols, cols)], out_ref.at[h, par, n], sems.at[h, par, n]
        )
        for h in range(H)
        for par in range(PAR)
        for n in range(C)
    ]
    for copy in copies:
        copy.start()
    for copy in copies:
        copy.wait()


def pick(batch_irrep, integrals):
    ab_rows, cols = integrals.shape[1:]
    return pl.pallas_call(
        pick_kernel,
        out_shape=jax.ShapeDtypeStruct((H, PAR, C, ab_rows, cols // H), integrals.dtype),
        in_specs=[pl.BlockSpec(memory_space=pltpu.SMEM), pl.BlockSpec(memory_space=pl.ANY)],
        out_specs=pl.BlockSpec(memory_space=pltpu.VMEM),
        scratch_shapes=[pltpu.SemaphoreType.DMA((H, PAR, C))],
        cost_estimate=pl.CostEstimate(flops=0, bytes_accessed=2**21, transcendentals=0),
        name="pick_blocks",
    )(batch_irrep, integrals)


def used_columns(irrep_ref, fill_ref, part, cols):
    x, h, core = (lax.axis_index(axis) for axis in ("x", "h", "c"))
    place = ((x * C + part) * H + h) * cols + lax.broadcasted_iota(jnp.int32, (1, cols), 1)
    return place < fill_ref[irrep_ref[core]]


def as_integers(tile, ab_rows):
    column = lax.broadcasted_iota(jnp.int32, (1, LANES), 1)
    peak = jnp.max(jnp.abs(tile), axis=1, keepdims=True)
    power = jnp.clip(jnp.ceil(jnp.log2(jnp.maximum(peak * 1.0001, 1e-37))), -111.0, 111.0)
    scaled = jnp.where(column == ab_rows, power, tile * jnp.exp2(TOP - power))
    return jnp.floor(scaled + 0.5).astype(jnp.int32).astype(jnp.int16)


def inside_block(tile, ab_rows):
    column = lax.broadcasted_iota(jnp.int32, (1, LANES), 1)
    return jnp.where(column < ab_rows, tile, jnp.zeros((), jnp.float32))


def early_kernel(irrep_ref, fill_ref, *refs):
    pairs, blocks_ref = refs[: 4 * C - 1], refs[4 * C - 1]
    out_ref, open_ref, left, right, held = refs[4 * C :]
    _, rows, cols = pairs[0].shape
    parts, ab_rows = blocks_ref.shape[1:3]
    y = lax.axis_index("y")
    for part in range(parts):
        used = used_columns(irrep_ref, fill_ref, part, cols)
        for at in range(Y):
            owner = owner_of(y, part, at)
            if part == 0 and at >= Y - 2:
                left[part, owner] = jnp.zeros((rows, cols), left.dtype)
            else:
                values = (pairs[:3] if part == 0 else pairs[3:])[at // 2][at % 2]
                left[part, owner] = jnp.where(used, values, jnp.zeros((), values.dtype))
    for at in range(QUAD):
        for part in range(parts):
            right[part, at, pl.ds(0, ab_rows)] = blocks_ref[at, part]
    for half in range(QUAD // 2):
        product = sum(
            lax.dot_general(
                left[part].reshape(Y * rows, cols),
                right[part, pl.ds(2 * half, 2)].reshape(2 * LANES, cols),
                (((1,), (1,)), ((), ())),
                preferred_element_type=jnp.float32,
            )
            for part in range(parts)
        )
        for side in range(2):
            tile = inside_block(product[:, side * LANES : (side + 1) * LANES], ab_rows)
            held[...] = tile.reshape(Y, rows, LANES)
            for late in range(2):
                open_ref[2 * half + side, late] = held[owner_of(y, 0, Y - 2 + late)]
            out_ref[2 * half + side] = as_integers(tile, ab_rows).reshape(Y, rows, LANES)


def late_kernel(irrep_ref, fill_ref, last_ref, blocks_ref, early_ref, open_ref, out_ref, right):
    _, rows, cols = last_ref.shape
    ab_rows = blocks_ref.shape[2]
    y = lax.axis_index("y")
    values = last_ref[...].reshape(2 * rows, cols)
    used = used_columns(irrep_ref, fill_ref, 0, cols)
    values = jnp.where(used, values, jnp.zeros((), values.dtype))
    for at in range(QUAD):
        right[at, pl.ds(0, ab_rows)] = blocks_ref[at, 0]
    out_ref[...] = early_ref[...]
    for half in range(QUAD // 2):
        product = lax.dot_general(
            values,
            right[pl.ds(2 * half, 2)].reshape(2 * LANES, cols),
            (((1,), (1,)), ((), ())),
            preferred_element_type=jnp.float32,
        )
        for side in range(2):
            tile = inside_block(product[:, side * LANES : (side + 1) * LANES], ab_rows)
            for late in range(2):
                whole = tile[late * rows : (late + 1) * rows] + open_ref[2 * half + side, late]
                out_ref[2 * half + side, owner_of(y, 0, Y - 2 + late)] = as_integers(whole, ab_rows)


def partial_ladder(batch_irrep, pair_fill, pairs, blocks):
    _, rows, cols = pairs[0].shape
    parts, ab_rows = blocks.shape[1:3]
    smem, vmem = pl.BlockSpec(memory_space=pltpu.SMEM), pl.BlockSpec(memory_space=pltpu.VMEM)
    whole = jax.ShapeDtypeStruct((QUAD, Y, rows, LANES), jnp.int16)
    early, still_open = pl.pallas_call(
        early_kernel,
        out_shape=(whole, jax.ShapeDtypeStruct((QUAD, 2, rows, LANES), jnp.float32)),
        in_specs=[smem] * 2 + [vmem] * len(pairs),
        out_specs=[vmem] * 2,
        scratch_shapes=[
            pltpu.VMEM((parts, Y, rows, cols), jnp.bfloat16),
            pltpu.VMEM((parts, QUAD, LANES, cols), jnp.bfloat16),
            pltpu.VMEM((Y, rows, LANES), jnp.float32),
        ],
        compiler_params=pltpu.CompilerParams(vmem_limit_bytes=24 * 2**20),
        cost_estimate=pl.CostEstimate(flops=2**30, bytes_accessed=6 * 2**20, transcendentals=0),
        name="early_ladder",
    )(batch_irrep, pair_fill, *pairs[:3], *pairs[4:], blocks)
    return pl.pallas_call(
        late_kernel,
        out_shape=whole,
        in_specs=[smem] * 2 + [vmem] * 4,
        out_specs=vmem,
        scratch_shapes=[pltpu.VMEM((QUAD, LANES, cols), jnp.bfloat16)],
        compiler_params=pltpu.CompilerParams(vmem_limit_bytes=24 * 2**20),
        cost_estimate=pl.CostEstimate(flops=2**28, bytes_accessed=2 * 2**20, transcendentals=0),
        name="late_ladder",
    )(batch_irrep, pair_fill, pairs[3], blocks, early, still_open)


def total_kernel(irrep_ref, fill_ref, parts_ref, out_ref):
    batches, ab_rows, _ = out_ref.shape
    rows = parts_ref.shape[1]
    place = lax.axis_index("y")
    for axis, size in (("za", ZA), ("h", H), ("par", PAR)):
        place = place * size + lax.axis_index(axis)
    ab = place * ab_rows + lax.broadcasted_iota(jnp.int32, (ab_rows, 1), 0)
    for n in range(batches):
        classes = []
        for par in range(PAR):
            total = jnp.zeros((rows, LANES), jnp.float32)
            for h in range(H):
                for x in range(X):
                    part = parts_ref[((h * PAR + par) * X + x) * C + n].astype(jnp.float32)
                    total += part * jnp.exp2(part[:, ab_rows : ab_rows + 1] - TOP)
            classes.append(total)
        eight = rows // (ZA * H)
        pieces = [
            classes[par][at * eight : (at + 1) * eight] for at in range(ZA * H) for par in range(PAR)
        ]
        turned = jnp.concatenate(pieces, axis=0).T[:ab_rows]
        out_ref[n] = jnp.where(ab < fill_ref[irrep_ref[n]], turned, jnp.zeros((), jnp.float32))


def total_ladder(batch_irrep, pair_fill, parts, batches, ab_rows):
    return pl.pallas_call(
        total_kernel,
        out_shape=jax.ShapeDtypeStruct((batches, ab_rows, PAR * parts.shape[1]), jnp.float32),
        in_specs=[pl.BlockSpec(memory_space=pltpu.SMEM)] * 2 + [pl.BlockSpec(memory_space=pltpu.VMEM)],
        out_specs=pl.BlockSpec(memory_space=pltpu.VMEM),
        cost_estimate=pl.CostEstimate(flops=2**20, bytes_accessed=2**20, transcendentals=0),
        name="total_ladder",
    )(batch_irrep, pair_fill, parts)


def on_device(amplitudes, integrals, batch_irrep, pair_fill):
    batches, own_pairs, cd_cols = amplitudes.shape
    ab_rows = integrals.shape[1]
    cols = cd_cols // H

    spread = amplitudes.reshape(batches, own_pairs, H, cols).transpose(2, 0, 1, 3)
    spread = jnp.broadcast_to(spread[None], (ZA, H, C, own_pairs, cols)).reshape(-1, own_pairs, cols)
    own = lax.all_to_all(spread, ("za", "h", "c"), 0, 0, tiled=True)
    own = own.reshape(ZA, H, C, own_pairs, cols).transpose(2, 0, 1, 3, 4).reshape(C, ZA * H * own_pairs, cols)

    picked = pick(batch_irrep, integrals).reshape(-1, ab_rows, cols)
    blocks = lax.all_to_all(picked, ("h", "par", "c"), 0, 0, tiled=True).reshape(QUAD, C, ab_rows, cols)

    pairs = [[], []]
    held = [own[0][None], own[1][None]]
    for step in range(4):
        for part in range(C):
            came = trade(held[part], (step + part) % 2)
            if step == 0:
                came = jnp.concatenate([held[part], came], axis=0)
            held[part] = came
            pairs[part].append(came)
    pairs = pairs[0] + pairs[1]

    partial = partial_ladder(batch_irrep, pair_fill, pairs, blocks)
    partial = partial.reshape(-1, *partial.shape[2:])
    parts = lax.all_to_all(partial, ("h", "par", "x", "c"), 0, 0, tiled=True)
    return total_ladder(batch_irrep, pair_fill, parts, batches, ab_rows).swapaxes(1, 2)


def solution(mesh):
    whole = Mesh(mesh.devices.reshape(Y, ZA, H, PAR, X, C), AXES)
    placed = (P(None, AXES[:4], AXES[4:]),) * 2 + (P(), P())
    return jax.shard_map(
        on_device, mesh=whole, in_specs=placed, out_specs=P(None, AXES[4:], AXES[:4]), check_vma=False
    )
```

```python
import functools

import jax
import jax.numpy as jnp
from jax import lax
from jax.experimental import pallas as pl
from jax.experimental.pallas import tpu as pltpu
from jax.sharding import Mesh, PartitionSpec as P

Y, ZA, H, PAR, X, C = 8, 4, 2, 2, 4, 2
AXES = ("y", "za", "h", "par", "x", "c")
QUAD = H * PAR
LANES = 128
TOP = 15


def trade(values, first):
    pairs = []
    for even in range(0, Y, 2):
        other = (even + 1 - 2 * first) % Y
        pairs += [(even, other), (other, even)]
    return lax.ppermute(values, "y", pairs)


def owner_of(y, part, at):
    step = (0, 1, -1, -2, 2, 3, -3, -4)[at]
    side = 1 - 2 * lax.rem(y + part, 2)
    return lax.rem(y + side * step + Y, Y)


def pick_kernel(irrep_ref, integrals_ref, out_ref, sems):
    cols = out_ref.shape[-1]
    copies = [
        pltpu.make_async_copy(
            integrals_ref.at[irrep_ref[n], :, pl.ds(h * cols, cols)], out_ref.at[h, par, n], sems.at[h, par, n]
        )
        for h in range(H)
        for par in range(PAR)
        for n in range(C)
    ]
    for copy in copies:
        copy.start()
    for copy in copies:
        copy.wait()


def pick(batch_irrep, integrals):
    ab_rows, cols = integrals.shape[1:]
    return pl.pallas_call(
        pick_kernel,
        out_shape=jax.ShapeDtypeStruct((H, PAR, C, ab_rows, cols // H), integrals.dtype),
        in_specs=[pl.BlockSpec(memory_space=pltpu.SMEM), pl.BlockSpec(memory_space=pl.ANY)],
        out_specs=pl.BlockSpec(memory_space=pltpu.VMEM),
        scratch_shapes=[pltpu.SemaphoreType.DMA((H, PAR, C))],
        cost_estimate=pl.CostEstimate(flops=0, bytes_accessed=2**21, transcendentals=0),
        name="pick_blocks",
    )(batch_irrep, integrals)


def used_columns(irrep_ref, fill_ref, part, cols):
    x, h, core = (lax.axis_index(axis) for axis in ("x", "h", "c"))
    place = ((x * C + part) * H + h) * cols + lax.broadcasted_iota(jnp.int32, (1, cols), 1)
    return place < fill_ref[irrep_ref[core]]


def as_integers(tile, ab_rows):
    column = lax.broadcasted_iota(jnp.int32, (1, LANES), 1)
    peak = jnp.max(jnp.abs(tile), axis=1, keepdims=True)
    power = jnp.clip(jnp.ceil(jnp.log2(jnp.maximum(peak * 1.0001, 1e-37))), -111.0, 111.0)
    scaled = jnp.where(column == ab_rows, power, tile * jnp.exp2(TOP - power))
    return jnp.floor(scaled + 0.5).astype(jnp.int32).astype(jnp.int16)


def used_rows(irrep_ref, fill_ref, block, tile, ab_rows):
    quad = lax.axis_index("y") * ZA + lax.axis_index("za")
    left_over = fill_ref[irrep_ref[lax.axis_index("c")]] - (quad * QUAD + block) * ab_rows
    column = lax.broadcasted_iota(jnp.int32, (1, LANES), 1)
    return jnp.where(column < jnp.minimum(left_over, ab_rows), tile, jnp.zeros((), jnp.float32))


def early_kernel(irrep_ref, fill_ref, *refs):
    pairs, blocks_ref = refs[: 4 * C - 1], refs[4 * C - 1]
    out_ref, open_ref, first, left, second, held = refs[4 * C :]
    right = (first, second)
    _, rows, cols = pairs[0].shape
    parts, ab_rows = blocks_ref.shape[1:3]
    y = lax.axis_index("y")
    for part in range(parts):
        used = used_columns(irrep_ref, fill_ref, part, cols)
        for at in range(Y):
            owner = owner_of(y, part, at)
            if part == 0 and at >= Y - 2:
                left[part, owner] = jnp.zeros((rows, cols), left.dtype)
            else:
                values = (pairs[:3] if part == 0 else pairs[3:])[at // 2][at % 2]
                left[part, owner] = jnp.where(used, values, jnp.zeros((), values.dtype))
    for at in range(QUAD):
        for part in range(parts):
            right[part][at, pl.ds(0, ab_rows)] = blocks_ref[at, part]
    for half in range(QUAD // 2):
        product = sum(
            lax.dot_general(
                left[part].reshape(Y * rows, cols),
                right[part][pl.ds(2 * half, 2)].reshape(2 * LANES, cols),
                (((1,), (1,)), ((), ())),
                preferred_element_type=jnp.float32,
            )
            for part in range(parts)
        )
        for side in range(2):
            tile = product[:, side * LANES : (side + 1) * LANES]
            tile = used_rows(irrep_ref, fill_ref, 2 * half + side, tile, ab_rows)
            held[...] = tile.reshape(Y, rows, LANES)
            for late in range(2):
                open_ref[2 * half + side, late] = held[owner_of(y, 0, Y - 2 + late)]
            out_ref[2 * half + side] = as_integers(tile, ab_rows).reshape(Y, rows, LANES)


def late_kernel(ab_rows, irrep_ref, fill_ref, last_ref, right, early_ref, open_ref, out_ref):
    _, rows, cols = last_ref.shape
    y = lax.axis_index("y")
    values = last_ref[...].reshape(2 * rows, cols)
    used = used_columns(irrep_ref, fill_ref, 0, cols)
    values = jnp.where(used, values, jnp.zeros((), values.dtype))
    out_ref[...] = early_ref[...]
    for half in range(QUAD // 2):
        product = lax.dot_general(
            values,
            right[pl.ds(2 * half, 2)].reshape(2 * LANES, cols),
            (((1,), (1,)), ((), ())),
            preferred_element_type=jnp.float32,
        )
        for side in range(2):
            tile = product[:, side * LANES : (side + 1) * LANES]
            tile = used_rows(irrep_ref, fill_ref, 2 * half + side, tile, ab_rows)
            for late in range(2):
                whole = tile[late * rows : (late + 1) * rows] + open_ref[2 * half + side, late]
                out_ref[2 * half + side, owner_of(y, 0, Y - 2 + late)] = as_integers(whole, ab_rows)


def partial_ladder(batch_irrep, pair_fill, pairs, blocks):
    _, rows, cols = pairs[0].shape
    parts, ab_rows = blocks.shape[1:3]
    smem, vmem = pl.BlockSpec(memory_space=pltpu.SMEM), pl.BlockSpec(memory_space=pltpu.VMEM)
    whole = jax.ShapeDtypeStruct((QUAD, Y, rows, LANES), jnp.int16)
    early, still_open, first = pl.pallas_call(
        early_kernel,
        out_shape=(
            whole,
            jax.ShapeDtypeStruct((QUAD, 2, rows, LANES), jnp.float32),
            jax.ShapeDtypeStruct((QUAD, LANES, cols), jnp.bfloat16),
        ),
        in_specs=[smem] * 2 + [vmem] * len(pairs),
        out_specs=[vmem] * 3,
        scratch_shapes=[
            pltpu.VMEM((parts, Y, rows, cols), jnp.bfloat16),
            pltpu.VMEM((QUAD, LANES, cols), jnp.bfloat16),
            pltpu.VMEM((Y, rows, LANES), jnp.float32),
        ],
        compiler_params=pltpu.CompilerParams(vmem_limit_bytes=24 * 2**20),
        cost_estimate=pl.CostEstimate(flops=2**30, bytes_accessed=6 * 2**20, transcendentals=0),
        name="early_ladder",
    )(batch_irrep, pair_fill, *pairs[:3], *pairs[4:], blocks)
    return pl.pallas_call(
        functools.partial(late_kernel, ab_rows),
        out_shape=whole,
        in_specs=[smem] * 2 + [vmem] * 4,
        out_specs=vmem,
        compiler_params=pltpu.CompilerParams(vmem_limit_bytes=24 * 2**20),
        cost_estimate=pl.CostEstimate(flops=2**28, bytes_accessed=2 * 2**20, transcendentals=0),
        name="late_ladder",
    )(batch_irrep, pair_fill, pairs[3], first, early, still_open)


def total_kernel(parts_ref, out_ref):
    batches, ab_rows, _ = out_ref.shape
    rows = parts_ref.shape[1]
    for n in range(batches):
        classes = []
        for par in range(PAR):
            total = jnp.zeros((rows, LANES), jnp.float32)
            for h in range(H):
                for x in range(X):
                    part = parts_ref[((h * PAR + par) * X + x) * C + n].astype(jnp.float32)
                    total += part * jnp.exp2(part[:, ab_rows : ab_rows + 1] - TOP)
            classes.append(total)
        eight = rows // (ZA * H)
        pieces = [
            classes[par][at * eight : (at + 1) * eight] for at in range(ZA * H) for par in range(PAR)
        ]
        out_ref[n] = jnp.concatenate(pieces, axis=0).T[:ab_rows]


def total_ladder(parts, batches, ab_rows):
    return pl.pallas_call(
        total_kernel,
        out_shape=jax.ShapeDtypeStruct((batches, ab_rows, PAR * parts.shape[1]), jnp.float32),
        in_specs=[pl.BlockSpec(memory_space=pltpu.VMEM)],
        out_specs=pl.BlockSpec(memory_space=pltpu.VMEM),
        cost_estimate=pl.CostEstimate(flops=2**20, bytes_accessed=2**20, transcendentals=0),
        name="total_ladder",
    )(parts)


def on_device(amplitudes, integrals, batch_irrep, pair_fill):
    batches, own_pairs, cd_cols = amplitudes.shape
    ab_rows = integrals.shape[1]
    cols = cd_cols // H

    spread = amplitudes.reshape(batches, own_pairs, H, cols).transpose(2, 0, 1, 3)
    spread = jnp.broadcast_to(spread[None], (ZA, H, C, own_pairs, cols)).reshape(-1, own_pairs, cols)
    own = lax.all_to_all(spread, ("za", "h", "c"), 0, 0, tiled=True)
    own = own.reshape(ZA, H, C, own_pairs, cols).transpose(2, 0, 1, 3, 4).reshape(C, ZA * H * own_pairs, cols)

    picked = pick(batch_irrep, integrals).reshape(-1, ab_rows, cols)
    blocks = lax.all_to_all(picked, ("h", "par", "c"), 0, 0, tiled=True).reshape(QUAD, C, ab_rows, cols)

    pairs = [[], []]
    held = [own[0][None], own[1][None]]
    for step in range(4):
        for part in range(C):
            came = trade(held[part], (step + part) % 2)
            if step == 0:
                came = jnp.concatenate([held[part], came], axis=0)
            held[part] = came
            pairs[part].append(came)
    pairs = pairs[0] + pairs[1]

    partial = partial_ladder(batch_irrep, pair_fill, pairs, blocks)
    partial = partial.reshape(-1, *partial.shape[2:])
    parts = lax.all_to_all(partial, ("h", "par", "x", "c"), 0, 0, tiled=True)
    return total_ladder(parts, batches, ab_rows).swapaxes(1, 2)


def solution(mesh):
    whole = Mesh(mesh.devices.reshape(Y, ZA, H, PAR, X, C), AXES)
    placed = (P(None, AXES[:4], AXES[4:]),) * 2 + (P(), P())
    return jax.shard_map(
        on_device, mesh=whole, in_specs=placed, out_specs=P(None, AXES[4:], AXES[:4]), check_vma=False
    )
```
